32 devices in a mesh: groups: 2 (over x), col: 16 (over z, y, core).
Axes of the slice: x: 2, y: 2, z: 4, core: 2. Of those that a mesh axis runs over, the one named last changes fastest.
Arguments:
- query_grad: bfloat16 [16384, 14336], P('groups', 'col'), parts along dimension 0, may hold values from -6 to 6
- out_basis: bfloat16 [16384, 2048], P(('groups', 'col')), parts along dimension 0, may hold values from -0.09375 to 0.09375
- in_basis: bfloat16 [28672, 384], P(('groups', 'col')), parts along dimension 0, may hold values from -0.0625 to 0.0625
- eigenvalues: float32 [4096, 384], P(('groups', 'col')), parts along dimension 0, may hold values from 0.05 to 20
- damping: float32 [2], P('groups'), parts along dimension 0, may hold values from 0.5 to 2
Outputs:
- ihvp: bfloat16 [16384, 14336], P('groups', 'col'), parts along dimension 0
The draws below stay inside these ranges and needn't reach their ends.
There are 2 independent parts, one for each index of `groups`. The reference program is written for one: setup_inputs(seed, part) draws one part's arguments, and reference() takes and returns one part's arrays. A program takes and returns all parts, laid end to end along the dimension named above; each array names one. Nothing has to cross between parts.
All inputs are finite; a program needn't handle non-finite values.
Results may differ from the reference program's by a relative error of at most 0.004.
Values may be sent and summed in bfloat16 or wider, within the bound.
A program may use at most 128 MiB of HBM per device.

```python
import math
import jax
import jax.numpy as jnp

D = 8192
DI = 14336
RO = 2048
RI = 384


def steps_of(own_key, extent, split, smallest, high):
    loudness = 1.0
    for dim, parts in split:
        heights = jax.random.uniform(jax.random.fold_in(jax.random.fold_in(own_key, 6), dim), (parts,), jnp.float32, smallest / len(split), high / len(split))
        loudness = loudness * jnp.repeat(jnp.exp(heights), extent[dim] // parts).reshape((-1,) + (1,) * (len(extent) - 1 - dim))
    return loudness


def gaussian(key, shape, scale, limit, shards=(), dtype=jnp.bfloat16):
    gain = steps_of(key, shape, shards, -0.22, 0.18) if shards else 1.0
    values = jax.random.normal(key, shape, jnp.float32) * scale * gain
    return jnp.minimum(jnp.maximum(values, -limit), limit).astype(dtype)


def setup_inputs(seed: int = 0, part: int = 0) -> dict:
    splits = jax.random.split(jax.random.key(seed), 6)
    part_splits = jax.random.split(jax.random.fold_in(splits[5], part), 6)
    return {
        "query_grad": gaussian(part_splits[0], (D, DI), 1.0, 6.0, ((1, 16),)),
        "out_basis": gaussian(part_splits[1], (D, RO), (D // 2) ** -0.5, 0.09375, ((0, 16),)),
        "in_basis": gaussian(part_splits[2], (DI, RI), (DI // 2) ** -0.5, 0.0625, ((0, 16),)),
        "eigenvalues": jnp.clip(jnp.exp(math.log(20.0) - 5.9914645 * jax.random.uniform(part_splits[3], (RO, RI), jnp.float32) ** steps_of(part_splits[3], (RO, RI), ((0, 16),), -0.2, 0.2)), 0.05, 20.0),
        "damping": jnp.clip(jnp.exp(jax.random.uniform(part_splits[4], (1,), jnp.float32, math.log(0.5), math.log(2.0))), 0.5, 2.0),
    }


def reference(query_grad, out_basis, in_basis, eigenvalues, damping):
    damp_value = damping[0]
    projected = jnp.dot(query_grad, in_basis, preferred_element_type=jnp.float32).astype(jnp.bfloat16)
    coords = jnp.dot(out_basis.T, projected, preferred_element_type=jnp.float32)
    factor = 1.0 / (eigenvalues + damp_value) - 1.0 / damp_value
    scaled = (coords * factor).astype(jnp.bfloat16)
    lifted = jnp.dot(out_basis, scaled, preferred_element_type=jnp.float32).astype(jnp.bfloat16)
    restored = jnp.dot(lifted, in_basis.T, preferred_element_type=jnp.float32)
    return (query_grad.astype(jnp.float32) / damp_value + restored).astype(jnp.bfloat16)
```

```python
import functools

import jax
import jax.numpy as jnp
from jax import lax
from jax.experimental import pallas as pl
from jax.experimental.pallas import tpu as pltpu
from jax.sharding import PartitionSpec as P

MESH = pl.DeviceIdType.MESH
SLOTS = 4


def rows_of(block, rows):
    return pl.ds(pl.multiple_of(block * rows, rows), rows)


def tile_of(rows):
    return 256 if rows % 256 == 0 else rows


class Place:
    def __init__(self, n):
        self.n = n
        self.depths = n // 4
        me = lax.axis_index("col")
        self.me = me
        self.z = me // 4
        self.y = (me // 2) % 2
        self.c = me % 2

    def index(self, z, y, c):
        return z * 4 + y * 2 + c

    def core_peer(self):
        return self.index(self.z, self.y, 1 - self.c)

    def side_peer(self):
        return self.index(self.z, 1 - self.y, self.c)

    def depth_peer(self, step):
        return self.index((self.z + step) % self.depths, self.y, self.c)


def remote(src, dst, send_sem, recv_sem, target):
    return pltpu.make_async_remote_copy(
        src_ref=src,
        dst_ref=dst,
        send_sem=send_sem,
        recv_sem=recv_sem,
        device_id={"col": target},
        device_id_type=MESH,
    )


def reduce_scatter(place, rows, produce, interlude, bufs):
    own, kept, csend, crecv, ysend, yrecv, zsend, zrecv, cs, cr, ys, yr, zs, zr = bufs
    nz = place.depths
    tile = tile_of(rows)

    def core_copy(i):
        return remote(csend.at[i], crecv.at[i], cs.at[i], cr.at[i], place.core_peer())

    def side_copy(k):
        return remote(ysend.at[k], yrecv.at[k], ys.at[k], yr.at[k], place.side_peer())

    def depth_copy(k):
        return remote(zsend.at[k], zrecv.at[k], zs.at[k], zr.at[k], place.depth_peer(k + 1))

    def tiles(body):
        @pl.loop(0, rows // tile)
        def _(t):
            body(pl.ds(pl.multiple_of(t * tile, tile), tile))

    produce(0, csend.at[0])
    core_copy(0).start()

    @pl.loop(0, nz)
    def _(k):
        produce(2 * k + 1, own)

        @pl.when(k + 1 < nz)
        def _():
            produce(2 * k + 2, csend.at[k + 1])
            core_copy(k + 1).start()

        core_copy(k).wait_recv()

        def add(r):
            ysend[k, r, :] = (own[r, :] + crecv[k, r, :].astype(jnp.float32)).astype(jnp.bfloat16)

        tiles(add)
        side_copy(k).start()

    @pl.loop(0, nz)
    def _(k):
        produce(2 * nz + 2 * k, csend.at[nz + k])
        core_copy(nz + k).start()
        produce(2 * nz + 2 * k + 1, kept.at[k])

    interlude()

    def total(k, r):
        return (
            kept[k, r, :]
            + crecv[nz + k, r, :].astype(jnp.float32)
            + yrecv[k, r, :].astype(jnp.float32)
        )

    @pl.loop(0, nz - 1)
    def _(k):
        core_copy(nz + k).wait_recv()
        side_copy(k).wait_recv()

        def add(r):
            zsend[k, r, :] = total(k, r).astype(jnp.bfloat16)

        tiles(add)
        depth_copy(k).start()

    core_copy(2 * nz - 1).wait_recv()
    side_copy(nz - 1).wait_recv()

    def last(r):
        own[r, :] = total(nz - 1, r)

    tiles(last)

    @pl.loop(0, nz - 1)
    def _(k):
        depth_copy(k).wait_recv()

        def add(r):
            own[r, :] += zrecv[k, r, :].astype(jnp.float32)

        tiles(add)

    @pl.loop(0, 2 * nz)
    def _(i):
        core_copy(i).wait_send()

    @pl.loop(0, nz)
    def _(k):
        side_copy(k).wait_send()

    @pl.loop(0, nz - 1)
    def _(k):
        depth_copy(k).wait_send()


def all_gather(place, rows, full, bufs):
    cs, cr, ys, yr, zs, zr = bufs
    nz = place.depths

    def at(block):
        return full.at[rows_of(block, rows)]

    def depth_copy(k, source_z):
        block = at(place.index(source_z, place.y, place.c))
        return remote(block, block, zs.at[k], zr.at[k], place.depth_peer(k))

    def side_copy(k, side):
        block = at(place.index((place.z - k + nz) % nz, side, place.c))
        return remote(block, block, ys.at[k], yr.at[k], place.side_peer())

    def core_copy(i, k, side, core):
        block = at(place.index((place.z - k + nz) % nz, side, core))
        return remote(block, block, cs.at[i], cr.at[i], place.core_peer())

    @pl.loop(1, nz)
    def _(k):
        depth_copy(k, place.z).start()

    @pl.loop(0, nz)
    def _(k):
        @pl.when(k > 0)
        def _():
            depth_copy(k, (place.z - k + nz) % nz).wait_recv()

        side_copy(k, place.y).start()
        core_copy(k, k, place.y, place.c).start()

    @pl.loop(0, nz)
    def _(k):
        side_copy(k, 1 - place.y).wait_recv()
        core_copy(nz + k, k, 1 - place.y, place.c).start()

    @pl.loop(0, nz)
    def _(k):
        core_copy(k, k, place.y, 1 - place.c).wait_recv()
        core_copy(nz + k, k, 1 - place.y, 1 - place.c).wait_recv()

    @pl.loop(1, nz)
    def _(k):
        depth_copy(k, place.z).wait_send()

    @pl.loop(0, nz)
    def _(k):
        side_copy(k, place.y).wait_send()
        core_copy(k, k, place.y, place.c).wait_send()
        core_copy(nz + k, k, 1 - place.y, place.c).wait_send()


def lift_kernel(
    n, query, out_basis, in_basis, eigenvalues, damping, lifted,
    slots, basis, turned, projected, scaled, slot_sems, basis_sem, *rest
):
    place = Place(n)
    nz = place.depths
    first, second, gather_scaled, gather_lifted = rest[:14], rest[14:28], rest[28:34], rest[34:40]
    rows = projected.shape[0]
    share = eigenvalues.shape[0]
    steps = 4 * nz

    def block_at(s):
        half = s // (2 * nz)
        k = (s % (2 * nz)) // 2
        side = (place.y + 1 + half) % 2
        core = (place.c + 1 + s) % 2
        return place.index((place.z + k + 1) % nz, side, core)

    def query_copy(s):
        return pltpu.make_async_copy(
            query.at[rows_of(block_at(s), rows)], slots.at[s % SLOTS], slot_sems.at[s % SLOTS]
        )

    basis_copy = pltpu.make_async_copy(out_basis, basis, basis_sem)

    @pl.loop(0, SLOTS - 1)
    def _(s):
        query_copy(s).start()

    barrier = pltpu.get_barrier_semaphore()
    for peer in (place.core_peer(), place.side_peer()):
        pl.semaphore_signal(barrier, inc=1, device_id={"col": peer}, device_id_type=MESH)

    @pl.loop(1, nz)
    def _(k):
        pl.semaphore_signal(
            barrier, inc=1, device_id={"col": place.depth_peer(k)}, device_id_type=MESH
        )

    pl.semaphore_wait(barrier, nz + 1)

    tile = tile_of(rows)

    def project(s, out):
        query_copy(s).wait()

        @pl.when(s + SLOTS - 1 < steps)
        def _():
            query_copy(s + SLOTS - 1).start()

        @pl.loop(0, rows // tile)
        def _(t):
            r = pl.ds(pl.multiple_of(t * tile, tile), tile)
            out[r, :] = jnp.dot(
                slots[s % SLOTS, r, :], in_basis[...], preferred_element_type=jnp.float32
            ).astype(out.dtype)

    basis_copy.start()

    def turn():
        basis_copy.wait()
        width = 256
        for j in range(basis.shape[1] // width):
            turned[j * width : (j + 1) * width, :] = basis[:, j * width : (j + 1) * width].T

    reduce_scatter(place, rows, project, turn, first)
    projected[...] = first[0][...].astype(jnp.bfloat16)

    def rotate(s, out):
        out[...] = jnp.dot(
            turned[rows_of(block_at(s), share), :],
            projected[...],
            preferred_element_type=jnp.float32,
        ).astype(out.dtype)

    reduce_scatter(place, share, rotate, lambda: None, second)
    damp_value = damping[...]
    factor = 1.0 / (eigenvalues[...] + damp_value) - 1.0 / damp_value
    scaled[rows_of(place.me, share), :] = (second[0][...] * factor).astype(jnp.bfloat16)
    all_gather(place, share, scaled, gather_scaled)

    @pl.loop(0, rows // tile)
    def _(t):
        r = pl.ds(pl.multiple_of(t * tile, tile), tile)
        o = pl.ds(pl.multiple_of(place.me * rows + t * tile, tile), tile)
        lifted[o, :] = jnp.dot(
            basis[r, :], scaled[...], preferred_element_type=jnp.float32
        ).astype(jnp.bfloat16)

    all_gather(place, rows, lifted, gather_lifted)


def scatter_scratch(nz, rows, width):
    block = (rows, width)
    dma = pltpu.SemaphoreType.DMA
    return [
        pltpu.VMEM(block, jnp.float32),
        pltpu.VMEM((nz, *block), jnp.float32),
        pltpu.VMEM((2 * nz, *block), jnp.bfloat16),
        pltpu.VMEM((2 * nz, *block), jnp.bfloat16),
        pltpu.VMEM((nz, *block), jnp.bfloat16),
        pltpu.VMEM((nz, *block), jnp.bfloat16),
        pltpu.VMEM((nz - 1, *block), jnp.bfloat16),
        pltpu.VMEM((nz - 1, *block), jnp.bfloat16),
        dma((2 * nz,)),
        dma((2 * nz,)),
        dma((nz,)),
        dma((nz,)),
        dma((nz - 1,)),
        dma((nz - 1,)),
    ]


def gather_scratch(nz):
    dma = pltpu.SemaphoreType.DMA
    return [dma((2 * nz,)), dma((2 * nz,)), dma((nz,)), dma((nz,)), dma((nz,)), dma((nz,))]


def lift(n, query_grad, out_basis, in_basis, eigenvalues, damping):
    nz = n // 4
    height, inner = query_grad.shape
    rows, kept = out_basis.shape
    width = in_basis.shape[1]
    share = eigenvalues.shape[0]
    vmem = pl.BlockSpec(memory_space=pltpu.VMEM)
    hbm = pl.BlockSpec(memory_space=pl.ANY)
    flops = 2 * height * inner * width + 4 * rows * kept * width
    return pl.pallas_call(
        functools.partial(lift_kernel, n),
        out_shape=jax.ShapeDtypeStruct((height, width), jnp.bfloat16),
        in_specs=[hbm, hbm, vmem, vmem, vmem],
        out_specs=vmem,
        scratch_shapes=[
            pltpu.VMEM((SLOTS, rows, inner), jnp.bfloat16),
            pltpu.VMEM((rows, kept), jnp.bfloat16),
            pltpu.VMEM((kept, rows), jnp.bfloat16),
            pltpu.VMEM((rows, width), jnp.bfloat16),
            pltpu.VMEM((kept, width), jnp.bfloat16),
            pltpu.SemaphoreType.DMA((SLOTS,)),
            pltpu.SemaphoreType.DMA,
            *scatter_scratch(nz, rows, width),
            *scatter_scratch(nz, share, width),
            *gather_scratch(nz),
            *gather_scratch(nz),
        ],
        compiler_params=pltpu.CompilerParams(
            collective_id=0, has_side_effects=True, vmem_limit_bytes=52 * 2**20
        ),
        cost_estimate=pl.CostEstimate(
            flops=flops, bytes_accessed=2 * height * inner, transcendentals=0
        ),
    )(query_grad, out_basis, in_basis, eigenvalues, damping.reshape(1, 1))


def on_device(n, query_grad, out_basis, in_basis, eigenvalues, damping):
    damp_value = damping[0]
    lifted = lift(n, query_grad, out_basis, in_basis, eigenvalues, damping)
    restored = lax.dot_general(
        lifted, in_basis, (((1,), (1,)), ((), ())), preferred_element_type=jnp.float32
    )
    return (query_grad.astype(jnp.float32) / damp_value + restored).astype(jnp.bfloat16)


def solution(mesh):
    in_specs = (
        P("groups", "col"),
        P(("groups", "col"), None),
        P(("groups", "col"), None),
        P(("groups", "col"), None),
        P("groups"),
    )
    out_specs = P("groups", "col")
    return jax.shard_map(
        functools.partial(on_device, mesh.shape["col"]),
        mesh=mesh,
        in_specs=in_specs,
        out_specs=out_specs,
        check_vma=False,
    )
```

```python
import functools

import jax
import jax.numpy as jnp
from jax import lax
from jax.experimental import pallas as pl
from jax.experimental.pallas import tpu as pltpu
from jax.sharding import PartitionSpec as P

MESH = pl.DeviceIdType.MESH
SLOTS = 4


def rows_of(block, rows):
    return pl.ds(pl.multiple_of(block * rows, rows), rows)


def tile_of(rows):
    return 256 if rows % 256 == 0 else rows


class Place:
    def __init__(self, n):
        self.n = n
        self.depths = n // 4
        me = lax.axis_index("col")
        self.me = me
        self.z = me // 4
        self.y = (me // 2) % 2
        self.c = me % 2

    def index(self, z, y, c):
        return z * 4 + y * 2 + c

    def core_peer(self):
        return self.index(self.z, self.y, 1 - self.c)

    def side_peer(self):
        return self.index(self.z, 1 - self.y, self.c)

    def depth_peer(self, step):
        return self.index((self.z + step + self.depths) % self.depths, self.y, self.c)

    def depth_at(self, k):
        z, last = self.z, self.depths - 1
        low = jnp.where(k < last - z, last - k, k - (last - z))
        high = jnp.where(k < z, k, last - (k - z))
        return jnp.where(k == last, z, jnp.where(2 * z < self.depths, low, high))


def remote(src, dst, send_sem, recv_sem, target):
    return pltpu.make_async_remote_copy(
        src_ref=src,
        dst_ref=dst,
        send_sem=send_sem,
        recv_sem=recv_sem,
        device_id={"col": target},
        device_id_type=MESH,
    )


def reduce_scatter(place, rows, produce, interlude, bufs):
    own, kept, csend, crecv, ysend, yrecv, zsend, zrecv, cs, cr, ys, yr, zs, zr = bufs
    nz = place.depths
    tile = tile_of(rows)

    def core_copy(i):
        return remote(csend.at[i], crecv.at[i], cs.at[i], cr.at[i], place.core_peer())

    def side_copy(k):
        return remote(ysend.at[k], yrecv.at[k], ys.at[k], yr.at[k], place.side_peer())

    def depth_copy(k, slot, step):
        return remote(zsend.at[k], zrecv.at[slot], zs.at[k], zr.at[slot], place.depth_peer(step))

    def arrived(slot):
        depth_copy(0, slot, 1).wait_recv()

    def tiles(body):
        @pl.loop(0, rows // tile)
        def _(t):
            body(pl.ds(pl.multiple_of(t * tile, tile), tile))

    produce(0, csend.at[0])
    core_copy(0).start()

    @pl.loop(0, nz)
    def _(k):
        produce(2 * k + 1, own)

        @pl.when(k + 1 < nz)
        def _():
            produce(2 * k + 2, csend.at[k + 1])
            core_copy(k + 1).start()

        core_copy(k).wait_recv()

        def add(r):
            ysend[k, r, :] = (own[r, :] + crecv[k, r, :].astype(jnp.float32)).astype(jnp.bfloat16)

        tiles(add)
        side_copy(k).start()

    @pl.loop(0, nz)
    def _(k):
        produce(2 * nz + 2 * k, csend.at[nz + k])
        core_copy(nz + k).start()
        produce(2 * nz + 2 * k + 1, kept.at[k])

    interlude()

    def total(k, r):
        return (
            kept[k, r, :]
            + crecv[nz + k, r, :].astype(jnp.float32)
            + yrecv[k, r, :].astype(jnp.float32)
        )

    @pl.loop(0, nz - 1)
    def _(k):
        core_copy(nz + k).wait_recv()
        side_copy(k).wait_recv()

        depth = place.depth_at(k)
        up = depth > place.z

        @pl.when(jnp.where(up, place.z > 0, place.z < nz - 1))
        def _():
            arrived(depth)

            def join(r):
                kept[k, r, :] += zrecv[depth, r, :].astype(jnp.float32)

            tiles(join)

        def add(r):
            zsend[k, r, :] = total(k, r).astype(jnp.bfloat16)

        tiles(add)

        @pl.when(up)
        def _():
            depth_copy(k, depth, 1).start()

        @pl.when(depth < place.z)
        def _():
            depth_copy(k, jnp.where(depth == place.z - 1, nz, depth), -1).start()

    core_copy(2 * nz - 1).wait_recv()
    side_copy(nz - 1).wait_recv()

    def last(r):
        own[r, :] = total(nz - 1, r)

    tiles(last)

    def finish(slot):
        arrived(slot)

        def add(r):
            own[r, :] += zrecv[slot, r, :].astype(jnp.float32)

        tiles(add)

    @pl.when(place.z > 0)
    def _():
        finish(place.z)

    @pl.when(place.z < nz - 1)
    def _():
        finish(nz)

    @pl.loop(0, 2 * nz)
    def _(i):
        core_copy(i).wait_send()

    @pl.loop(0, nz)
    def _(k):
        side_copy(k).wait_send()

    @pl.loop(0, nz - 1)
    def _(k):
        depth_copy(k, k, 1).wait_send()


def all_gather(place, rows, full, bufs):
    cs, cr, ys, yr, zs, zr = bufs
    nz = place.depths

    def at(block):
        return full.at[rows_of(block, rows)]

    def depth_copy(distance, step):
        block = at(place.index(place.z - step * (distance - 1), place.y, place.c))
        i = distance if step == 1 else nz + distance
        return remote(block, block, zs.at[i], zr.at[i], place.depth_peer(step))

    def depth_arrived(distance, step):
        block = at(place.index(place.z - step * distance, place.y, place.c))
        i = distance if step == 1 else nz + distance
        remote(block, block, zs.at[i], zr.at[i], place.depth_peer(step)).wait_recv()

    def side_copy(z, side):
        block = at(place.index(z, side, place.c))
        return remote(block, block, ys.at[z], yr.at[z], place.side_peer())

    def core_copy(i, z, side, core):
        block = at(place.index(z, side, core))
        return remote(block, block, cs.at[i], cr.at[i], place.core_peer())

    def share(z):
        side_copy(z, place.y).start()
        core_copy(z, z, place.y, place.c).start()

    def pass_on(z):
        side_copy(z, 1 - place.y).wait_recv()
        core_copy(nz + z, z, 1 - place.y, place.c).start()

    def has_source(distance, step):
        return place.z >= distance if step == 1 else place.z + distance < nz

    def has_next(step):
        return place.z < nz - 1 if step == 1 else place.z > 0

    for step in (1, -1):

        @pl.when(has_next(step))
        def _(step=step):
            depth_copy(1, step).start()

    share(place.z)

    @pl.loop(1, nz)
    def _(k):
        for step in (1, -1):

            @pl.when(has_source(k, step))
            def _(step=step):
                depth_arrived(k, step)

                @pl.when(has_next(step))
                def _():
                    depth_copy(k + 1, step).start()

                share(place.z - step * k)

    pass_on(place.z)

    @pl.loop(1, nz)
    def _(k):
        for step in (1, -1):

            @pl.when(has_source(k, step))
            def _(step=step):
                pass_on(place.z - step * k)

    @pl.loop(0, nz)
    def _(z):
        core_copy(z, z, place.y, 1 - place.c).wait_recv()
        core_copy(nz + z, z, 1 - place.y, 1 - place.c).wait_recv()
        side_copy(z, place.y).wait_send()
        core_copy(z, z, place.y, place.c).wait_send()
        core_copy(nz + z, z, 1 - place.y, place.c).wait_send()

    @pl.loop(0, nz - 1)
    def _(k):
        for step in (1, -1):

            @pl.when(jnp.logical_and(jnp.logical_or(k == 0, has_source(k, step)), has_next(step)))
            def _(step=step):
                depth_copy(k + 1, step).wait_send()


def lift_kernel(
    n, query, out_basis, in_basis, eigenvalues, damping, lifted,
    slots, basis, turned, projected, scaled, slot_sems, basis_sem, *rest
):
    place = Place(n)
    nz = place.depths
    first, second, gather_scaled, gather_lifted = rest[:14], rest[14:28], rest[28:34], rest[34:40]
    rows = projected.shape[0]
    share = eigenvalues.shape[0]
    steps = 4 * nz

    def block_at(s):
        half = s // (2 * nz)
        k = (s % (2 * nz)) // 2
        side = (place.y + 1 + half) % 2
        core = (place.c + 1 + s) % 2
        return place.index(place.depth_at(k), side, core)

    def query_copy(s):
        return pltpu.make_async_copy(
            query.at[rows_of(block_at(s), rows)], slots.at[s % SLOTS], slot_sems.at[s % SLOTS]
        )

    basis_copy = pltpu.make_async_copy(out_basis, basis, basis_sem)

    @pl.loop(0, SLOTS - 1)
    def _(s):
        query_copy(s).start()

    barrier = pltpu.get_barrier_semaphore()
    for peer in (place.core_peer(), place.side_peer()):
        pl.semaphore_signal(barrier, inc=1, device_id={"col": peer}, device_id_type=MESH)

    @pl.loop(1, nz)
    def _(k):
        pl.semaphore_signal(
            barrier, inc=1, device_id={"col": place.depth_peer(k)}, device_id_type=MESH
        )

    pl.semaphore_wait(barrier, nz + 1)

    tile = tile_of(rows)

    def project(s, out):
        query_copy(s).wait()

        @pl.when(s + SLOTS - 1 < steps)
        def _():
            query_copy(s + SLOTS - 1).start()

        @pl.loop(0, rows // tile)
        def _(t):
            r = pl.ds(pl.multiple_of(t * tile, tile), tile)
            out[r, :] = jnp.dot(
                slots[s % SLOTS, r, :], in_basis[...], preferred_element_type=jnp.float32
            ).astype(out.dtype)

    basis_copy.start()

    def turn():
        basis_copy.wait()
        width = 256
        for j in range(basis.shape[1] // width):
            turned[j * width : (j + 1) * width, :] = basis[:, j * width : (j + 1) * width].T

    reduce_scatter(place, rows, project, turn, first)
    projected[...] = first[0][...].astype(jnp.bfloat16)

    def rotate(s, out):
        out[...] = jnp.dot(
            turned[rows_of(block_at(s), share), :],
            projected[...],
            preferred_element_type=jnp.float32,
        ).astype(out.dtype)

    reduce_scatter(place, share, rotate, lambda: None, second)
    damp_value = damping[...]
    factor = 1.0 / (eigenvalues[...] + damp_value) - 1.0 / damp_value
    scaled[rows_of(place.me, share), :] = (second[0][...] * factor).astype(jnp.bfloat16)
    all_gather(place, share, scaled, gather_scaled)

    @pl.loop(0, rows // tile)
    def _(t):
        r = pl.ds(pl.multiple_of(t * tile, tile), tile)
        o = pl.ds(pl.multiple_of(place.me * rows + t * tile, tile), tile)
        lifted[o, :] = jnp.dot(
            basis[r, :], scaled[...], preferred_element_type=jnp.float32
        ).astype(jnp.bfloat16)

    all_gather(place, rows, lifted, gather_lifted)


def scatter_scratch(nz, rows, width):
    block = (rows, width)
    dma = pltpu.SemaphoreType.DMA
    return [
        pltpu.VMEM(block, jnp.float32),
        pltpu.VMEM((nz, *block), jnp.float32),
        pltpu.VMEM((2 * nz, *block), jnp.bfloat16),
        pltpu.VMEM((2 * nz, *block), jnp.bfloat16),
        pltpu.VMEM((nz, *block), jnp.bfloat16),
        pltpu.VMEM((nz, *block), jnp.bfloat16),
        pltpu.VMEM((nz - 1, *block), jnp.bfloat16),
        pltpu.VMEM((nz + 1, *block), jnp.bfloat16),
        dma((2 * nz,)),
        dma((2 * nz,)),
        dma((nz,)),
        dma((nz,)),
        dma((nz - 1,)),
        dma((nz + 1,)),
    ]


def gather_scratch(nz):
    dma = pltpu.SemaphoreType.DMA
    return [dma((2 * nz,)), dma((2 * nz,)), dma((nz,)), dma((nz,)), dma((2 * nz,)), dma((2 * nz,))]


def lift(n, query_grad, out_basis, in_basis, eigenvalues, damping):
    nz = n // 4
    height, inner = query_grad.shape
    rows, kept = out_basis.shape
    width = in_basis.shape[1]
    share = eigenvalues.shape[0]
    vmem = pl.BlockSpec(memory_space=pltpu.VMEM)
    hbm = pl.BlockSpec(memory_space=pl.ANY)
    flops = 2 * height * inner * width + 4 * rows * kept * width
    return pl.pallas_call(
        functools.partial(lift_kernel, n),
        out_shape=jax.ShapeDtypeStruct((height, width), jnp.bfloat16),
        in_specs=[hbm, hbm, vmem, vmem, vmem],
        out_specs=vmem,
        scratch_shapes=[
            pltpu.VMEM((SLOTS, rows, inner), jnp.bfloat16),
            pltpu.VMEM((rows, kept), jnp.bfloat16),
            pltpu.VMEM((kept, rows), jnp.bfloat16),
            pltpu.VMEM((rows, width), jnp.bfloat16),
            pltpu.VMEM((kept, width), jnp.bfloat16),
            pltpu.SemaphoreType.DMA((SLOTS,)),
            pltpu.SemaphoreType.DMA,
            *scatter_scratch(nz, rows, width),
            *scatter_scratch(nz, share, width),
            *gather_scratch(nz),
            *gather_scratch(nz),
        ],
        compiler_params=pltpu.CompilerParams(
            collective_id=0, has_side_effects=True, vmem_limit_bytes=52 * 2**20
        ),
        cost_estimate=pl.CostEstimate(
            flops=flops, bytes_accessed=2 * height * inner, transcendentals=0
        ),
    )(query_grad, out_basis, in_basis, eigenvalues, damping.reshape(1, 1))


def on_device(n, query_grad, out_basis, in_basis, eigenvalues, damping):
    damp_value = damping[0]
    lifted = lift(n, query_grad, out_basis, in_basis, eigenvalues, damping)
    restored = lax.dot_general(
        lifted, in_basis, (((1,), (1,)), ((), ())), preferred_element_type=jnp.float32
    )
    return (query_grad.astype(jnp.float32) / damp_value + restored).astype(jnp.bfloat16)


def solution(mesh):
    in_specs = (
        P("groups", "col"),
        P(("groups", "col"), None),
        P(("groups", "col"), None),
        P(("groups", "col"), None),
        P("groups"),
    )
    out_specs = P("groups", "col")
    return jax.shard_map(
        functools.partial(on_device, mesh.shape["col"]),
        mesh=mesh,
        in_specs=in_specs,
        out_specs=out_specs,
        check_vma=False,
    )
```

```python
import functools

import jax
import jax.numpy as jnp
from jax import lax
from jax.experimental import pallas as pl
from jax.experimental.pallas import tpu as pltpu
from jax.sharding import PartitionSpec as P

MESH = pl.DeviceIdType.MESH
SLOTS = 4


def rows_of(block, rows):
    return pl.ds(pl.multiple_of(block * rows, rows), rows)


def tile_of(rows):
    return 256 if rows % 256 == 0 else rows


class Place:
    def __init__(self, n):
        self.n = n
        self.depths = n // 4
        me = lax.axis_index("col")
        self.me = me
        self.z = me // 4
        self.y = (me // 2) % 2
        self.c = me % 2

    def index(self, z, y, c):
        return z * 4 + y * 2 + c

    def core_peer(self):
        return self.index(self.z, self.y, 1 - self.c)

    def side_peer(self):
        return self.index(self.z, 1 - self.y, self.c)

    def depth_peer(self, step):
        return self.index((self.z + step + self.depths) % self.depths, self.y, self.c)

    def depth_at(self, k):
        z, last = self.z, self.depths - 1
        low = jnp.where(k < last - z, last - k, k - (last - z))
        high = jnp.where(k < z, k, last - (k - z))
        return jnp.where(k == last, z, jnp.where(2 * z < self.depths, low, high))


def remote(src, dst, send_sem, recv_sem, target):
    return pltpu.make_async_remote_copy(
        src_ref=src,
        dst_ref=dst,
        send_sem=send_sem,
        recv_sem=recv_sem,
        device_id={"col": target},
        device_id_type=MESH,
    )


def reduce_scatter(place, rows, produce, interlude, bufs):
    own, kept, csend, crecv, ysend, yrecv, zsend, zrecv, cs, cr, ys, yr, zs, zr = bufs
    nz = place.depths
    tile = tile_of(rows)

    def core_copy(i):
        return remote(csend.at[i], crecv.at[i], cs.at[i], cr.at[i], place.core_peer())

    def side_copy(k):
        return remote(ysend.at[k], yrecv.at[k], ys.at[k], yr.at[k], place.side_peer())

    def depth_copy(k, slot, step):
        return remote(zsend.at[k], zrecv.at[slot], zs.at[k], zr.at[slot], place.depth_peer(step))

    def arrived(slot):
        depth_copy(0, slot, 1).wait_recv()

    def tiles(body):
        @pl.loop(0, rows // tile)
        def _(t):
            body(pl.ds(pl.multiple_of(t * tile, tile), tile))

    produce(0, csend.at[0])
    core_copy(0).start()

    @pl.loop(0, nz)
    def _(k):
        produce(2 * k + 1, own)

        @pl.when(k + 1 < nz)
        def _():
            produce(2 * k + 2, csend.at[k + 1])
            core_copy(k + 1).start()

        core_copy(k).wait_recv()

        def add(r):
            ysend[k, r, :] = (own[r, :] + crecv[k, r, :].astype(jnp.float32)).astype(jnp.bfloat16)

        tiles(add)
        side_copy(k).start()

    @pl.loop(0, nz)
    def _(k):
        produce(2 * nz + 2 * k, csend.at[nz + k])
        core_copy(nz + k).start()
        produce(2 * nz + 2 * k + 1, kept.at[k])

    interlude()

    def total(k, r):
        return (
            kept[k, r, :]
            + crecv[nz + k, r, :].astype(jnp.float32)
            + yrecv[k, r, :].astype(jnp.float32)
        )

    @pl.loop(0, nz - 1)
    def _(k):
        core_copy(nz + k).wait_recv()
        side_copy(k).wait_recv()

        depth = place.depth_at(k)
        up = depth > place.z

        @pl.when(jnp.where(up, place.z > 0, place.z < nz - 1))
        def _():
            arrived(depth)

            def join(r):
                kept[k, r, :] += zrecv[depth, r, :].astype(jnp.float32)

            tiles(join)

        def add(r):
            zsend[k, r, :] = total(k, r).astype(jnp.bfloat16)

        tiles(add)

        @pl.when(up)
        def _():
            depth_copy(k, depth, 1).start()

        @pl.when(depth < place.z)
        def _():
            depth_copy(k, jnp.where(depth == place.z - 1, nz, depth), -1).start()

    core_copy(2 * nz - 1).wait_recv()
    side_copy(nz - 1).wait_recv()

    def last(r):
        own[r, :] = total(nz - 1, r)

    tiles(last)

    def finish(slot):
        arrived(slot)

        def add(r):
            own[r, :] += zrecv[slot, r, :].astype(jnp.float32)

        tiles(add)

    @pl.when(place.z > 0)
    def _():
        finish(place.z)

    @pl.when(place.z < nz - 1)
    def _():
        finish(nz)

    @pl.loop(0, 2 * nz)
    def _(i):
        core_copy(i).wait_send()

    @pl.loop(0, nz)
    def _(k):
        side_copy(k).wait_send()

    @pl.loop(0, nz - 1)
    def _(k):
        depth_copy(k, k, 1).wait_send()


def all_gather(place, rows, full, bufs):
    cs, cr, ys, yr, zs, zr = bufs
    nz = place.depths

    def at(block):
        return full.at[rows_of(block, rows)]

    def depth_copy(distance, step):
        block = at(place.index(place.z - step * (distance - 1), place.y, place.c))
        i = distance if step == 1 else nz + distance
        return remote(block, block, zs.at[i], zr.at[i], place.depth_peer(step))

    def depth_arrived(distance, step):
        block = at(place.index(place.z - step * distance, place.y, place.c))
        i = distance if step == 1 else nz + distance
        remote(block, block, zs.at[i], zr.at[i], place.depth_peer(step)).wait_recv()

    def side_copy(z, side):
        block = at(place.index(z, side, place.c))
        return remote(block, block, ys.at[z], yr.at[z], place.side_peer())

    def core_copy(i, z, side, core):
        block = at(place.index(z, side, core))
        return remote(block, block, cs.at[i], cr.at[i], place.core_peer())

    def share(z):
        side_copy(z, place.y).start()
        core_copy(z, z, place.y, place.c).start()

    def pass_on(z):
        side_copy(z, 1 - place.y).wait_recv()
        core_copy(nz + z, z, 1 - place.y, place.c).start()

    def has_source(distance, step):
        return place.z >= distance if step == 1 else place.z + distance < nz

    def has_next(step):
        return place.z < nz - 1 if step == 1 else place.z > 0

    for step in (1, -1):

        @pl.when(has_next(step))
        def _(step=step):
            depth_copy(1, step).start()

    share(place.z)

    @pl.loop(1, nz)
    def _(k):
        for step in (1, -1):

            @pl.when(has_source(k, step))
            def _(step=step):
                depth_arrived(k, step)

                @pl.when(has_next(step))
                def _():
                    depth_copy(k + 1, step).start()

                share(place.z - step * k)

    pass_on(place.z)

    @pl.loop(1, nz)
    def _(k):
        for step in (1, -1):

            @pl.when(has_source(k, step))
            def _(step=step):
                pass_on(place.z - step * k)

    @pl.loop(0, nz)
    def _(z):
        core_copy(z, z, place.y, 1 - place.c).wait_recv()
        core_copy(nz + z, z, 1 - place.y, 1 - place.c).wait_recv()
        side_copy(z, place.y).wait_send()
        core_copy(z, z, place.y, place.c).wait_send()
        core_copy(nz + z, z, 1 - place.y, place.c).wait_send()

    @pl.loop(0, nz - 1)
    def _(k):
        for step in (1, -1):

            @pl.when(jnp.logical_and(jnp.logical_or(k == 0, has_source(k, step)), has_next(step)))
            def _(step=step):
                depth_copy(k + 1, step).wait_send()


def lift_kernel(
    n, query, out_basis, in_source, eigen_source, damping, lifted,
    slots, basis, turned, projected, scaled, in_basis, eigenvalues,
    slot_sems, basis_sem, in_sem, eigen_sem, *rest
):
    place = Place(n)
    nz = place.depths
    first, second, gather_scaled, gather_lifted = rest[:14], rest[14:28], rest[28:34], rest[34:40]
    rows = projected.shape[0]
    share = eigenvalues.shape[0]
    steps = 4 * nz

    def block_at(s):
        half = s // (2 * nz)
        k = (s % (2 * nz)) // 2
        side = (place.y + 1 + half) % 2
        core = (place.c + 1 + s) % 2
        return place.index(place.depth_at(k), side, core)

    def query_copy(s):
        return pltpu.make_async_copy(
            query.at[rows_of(block_at(s), rows)], slots.at[s % SLOTS], slot_sems.at[s % SLOTS]
        )

    basis_copy = pltpu.make_async_copy(out_basis, basis, basis_sem)
    in_copy = pltpu.make_async_copy(in_source, in_basis, in_sem)
    eigen_copy = pltpu.make_async_copy(eigen_source, eigenvalues, eigen_sem)
    in_copy.start()

    @pl.loop(0, SLOTS - 1)
    def _(s):
        query_copy(s).start()

    barrier = pltpu.get_barrier_semaphore()
    for peer in (place.core_peer(), place.side_peer()):
        pl.semaphore_signal(barrier, inc=1, device_id={"col": peer}, device_id_type=MESH)

    @pl.loop(1, nz)
    def _(k):
        pl.semaphore_signal(
            barrier, inc=1, device_id={"col": place.depth_peer(k)}, device_id_type=MESH
        )

    pl.semaphore_wait(barrier, nz + 1)

    tile = tile_of(rows)

    def project(s, out):
        query_copy(s).wait()

        @pl.when(s + SLOTS - 1 < steps)
        def _():
            query_copy(s + SLOTS - 1).start()

        @pl.loop(0, rows // tile)
        def _(t):
            r = pl.ds(pl.multiple_of(t * tile, tile), tile)
            out[r, :] = jnp.dot(
                slots[s % SLOTS, r, :], in_basis[...], preferred_element_type=jnp.float32
            ).astype(out.dtype)

    basis_copy.start()
    eigen_copy.start()
    in_copy.wait()

    def turn():
        basis_copy.wait()
        eigen_copy.wait()
        width = 256
        for j in range(basis.shape[1] // width):
            turned[j * width : (j + 1) * width, :] = basis[:, j * width : (j + 1) * width].T

    reduce_scatter(place, rows, project, turn, first)
    projected[...] = first[0][...].astype(jnp.bfloat16)

    def rotate(s, out):
        out[...] = jnp.dot(
            turned[rows_of(block_at(s), share), :],
            projected[...],
            preferred_element_type=jnp.float32,
        ).astype(out.dtype)

    reduce_scatter(place, share, rotate, lambda: None, second)
    damp_value = damping[...]
    factor = 1.0 / (eigenvalues[...] + damp_value) - 1.0 / damp_value
    scaled[rows_of(place.me, share), :] = (second[0][...] * factor).astype(jnp.bfloat16)
    all_gather(place, share, scaled, gather_scaled)

    @pl.loop(0, rows // tile)
    def _(t):
        r = pl.ds(pl.multiple_of(t * tile, tile), tile)
        o = pl.ds(pl.multiple_of(place.me * rows + t * tile, tile), tile)
        lifted[o, :] = jnp.dot(
            basis[r, :], scaled[...], preferred_element_type=jnp.float32
        ).astype(jnp.bfloat16)

    all_gather(place, rows, lifted, gather_lifted)


def scatter_scratch(nz, rows, width):
    block = (rows, width)
    dma = pltpu.SemaphoreType.DMA
    return [
        pltpu.VMEM(block, jnp.float32),
        pltpu.VMEM((nz, *block), jnp.float32),
        pltpu.VMEM((2 * nz, *block), jnp.bfloat16),
        pltpu.VMEM((2 * nz, *block), jnp.bfloat16),
        pltpu.VMEM((nz, *block), jnp.bfloat16),
        pltpu.VMEM((nz, *block), jnp.bfloat16),
        pltpu.VMEM((nz - 1, *block), jnp.bfloat16),
        pltpu.VMEM((nz + 1, *block), jnp.bfloat16),
        dma((2 * nz,)),
        dma((2 * nz,)),
        dma((nz,)),
        dma((nz,)),
        dma((nz - 1,)),
        dma((nz + 1,)),
    ]


def gather_scratch(nz):
    dma = pltpu.SemaphoreType.DMA
    return [dma((2 * nz,)), dma((2 * nz,)), dma((nz,)), dma((nz,)), dma((2 * nz,)), dma((2 * nz,))]


def lift(n, query_grad, out_basis, in_basis, eigenvalues, damping):
    nz = n // 4
    height, inner = query_grad.shape
    rows, kept = out_basis.shape
    width = in_basis.shape[1]
    share = eigenvalues.shape[0]
    vmem = pl.BlockSpec(memory_space=pltpu.VMEM)
    hbm = pl.BlockSpec(memory_space=pl.ANY)
    flops = 2 * height * inner * width + 4 * rows * kept * width
    return pl.pallas_call(
        functools.partial(lift_kernel, n),
        out_shape=jax.ShapeDtypeStruct((height, width), jnp.bfloat16),
        in_specs=[hbm, hbm, hbm, hbm, vmem],
        out_specs=vmem,
        scratch_shapes=[
            pltpu.VMEM((SLOTS, rows, inner), jnp.bfloat16),
            pltpu.VMEM((rows, kept), jnp.bfloat16),
            pltpu.VMEM((kept, rows), jnp.bfloat16),
            pltpu.VMEM((rows, width), jnp.bfloat16),
            pltpu.VMEM((kept, width), jnp.bfloat16),
            pltpu.VMEM((inner, width), jnp.bfloat16),
            pltpu.VMEM((share, width), jnp.float32),
            pltpu.SemaphoreType.DMA((SLOTS,)),
            pltpu.SemaphoreType.DMA,
            pltpu.SemaphoreType.DMA,
            pltpu.SemaphoreType.DMA,
            *scatter_scratch(nz, rows, width),
            *scatter_scratch(nz, share, width),
            *gather_scratch(nz),
            *gather_scratch(nz),
        ],
        compiler_params=pltpu.CompilerParams(
            collective_id=0, has_side_effects=True, vmem_limit_bytes=52 * 2**20
        ),
        cost_estimate=pl.CostEstimate(
            flops=flops, bytes_accessed=2 * height * inner, transcendentals=0
        ),
    )(query_grad, out_basis, in_basis, eigenvalues, damping.reshape(1, 1))


def on_device(n, query_grad, out_basis, in_basis, eigenvalues, damping):
    damp_value = damping[0]
    lifted = lift(n, query_grad, out_basis, in_basis, eigenvalues, damping)
    restored = lax.dot_general(
        lifted, in_basis, (((1,), (1,)), ((), ())), preferred_element_type=jnp.float32
    )
    return (query_grad.astype(jnp.float32) / damp_value + restored).astype(jnp.bfloat16)


def solution(mesh):
    in_specs = (
        P("groups", "col"),
        P(("groups", "col"), None),
        P(("groups", "col"), None),
        P(("groups", "col"), None),
        P("groups"),
    )
    out_specs = P("groups", "col")
    return jax.shard_map(
        functools.partial(on_device, mesh.shape["col"]),
        mesh=mesh,
        in_specs=in_specs,
        out_specs=out_specs,
        check_vma=False,
    )
```
